32 devices in a mesh: grp: 2 (over y), row: 4 (over z), vec: 2 (over x), sub: 2 (over core).
Axes of the slice: x: 2, y: 2, z: 4, core: 2. Of those that a mesh axis runs over, the one named last changes fastest.
Arguments:
- chol_vectors: float32 [64, 1280, 1280], P(('grp', 'vec'), ('row', 'sub')), parts along dimension 0, may hold values from -90 to 90, as said below
- orbitals: float32 [2560, 1280], P(('grp', 'row', 'sub')), parts along dimension 0, may hold values from -0.15625 to 0.15625
- one_body: float32 [2560, 1280], P(('grp', 'row', 'sub')), parts along dimension 0, may hold values from -7.5 to 7.5, as said below
Outputs:
- rotated: float32 [64, 1280, 1280], P(('grp', 'vec'), ('row', 'sub')), parts along dimension 0
- onebody_rot: float32 [2560, 1280], P(('grp', 'row', 'sub')), parts along dimension 0
- diag_mean: float32 [2560], P(('grp', 'row', 'sub')), parts along dimension 0
The draws below stay inside these ranges and needn't reach their ends.
There are 2 independent parts, one for each index of `grp`. The reference program is written for one: setup_inputs(seed, part) draws one part's arguments, and reference() takes and returns one part's arrays. A program takes and returns all parts, laid end to end along the dimension named above; each array names one. Nothing has to cross between parts.
Inputs may be any that keep to these rules, and one draw needn't show every extreme that they name: `chol_vectors`: each vector is a symmetric matrix. `one_body`: a symmetric matrix.
All inputs are finite; a program needn't handle non-finite values.
Results may differ from the reference program's by a relative error of at most 0.00014.
Values sent between devices are 32-bit elements; how exact they have to be, the bound alone decides.
A program may use at most 192 MiB of HBM per device.

```python
import jax
import jax.numpy as jnp
from jax import lax

N = 1280
G = 32


def draw_chol_vectors(key, part):
    key = jax.random.fold_in(key, 11)
    key_base, key_jit = jax.random.split(key)
    base = jnp.clip(jax.random.normal(key_base, (G, N, N)), -5.0, 5.0)
    sym_base = (base + jnp.swapaxes(base, 1, 2)) * 0.70710678
    rising = jnp.power(10.0, jnp.arange(G, dtype=jnp.float32) / max(G - 1, 1))
    jitter = jax.random.uniform(key_jit, (G,), minval=0.8, maxval=1.25)
    return (sym_base * (rising * jitter)[:, None, None]).astype(jnp.float32)


def draw_one_body(key, part):
    key = jax.random.fold_in(key, 23)
    base = jnp.clip(jax.random.normal(key, (N, N)), -5.0, 5.0)
    return ((base + base.T) * 0.70710678).astype(jnp.float32)


def levels(own_key, extent, shards, smallest, high):
    def one(dim, parts):
        heights = jax.random.uniform(jax.random.fold_in(jax.random.fold_in(own_key, 6), dim), (parts,), jnp.float32, smallest / len(shards), high / len(shards))
        return jnp.repeat(jnp.exp(heights), extent[dim] // parts).reshape((-1,) + (1,) * (len(extent) - dim - 1))

    loudness = one(*shards[0])
    for cut in shards[1:]:
        loudness = loudness * one(*cut)
    return loudness


def gaussian(rng, extent, width, bound, shards=(), kind=jnp.bfloat16):
    factor_of = levels(rng, extent, shards, -0.22, 0.18) if shards else 1.0
    result = jax.random.normal(rng, extent, jnp.float32) * width * factor_of
    return jnp.minimum(jnp.maximum(result, -bound), bound).astype(kind)


def setup_inputs(seed: int = 0, part: int = 0) -> dict:
    streams_of = jax.random.split(jax.random.key(seed), 4)
    own_keys = jax.random.split(jax.random.fold_in(streams_of[3], part), 4)
    chol_vectors = draw_chol_vectors(jax.random.fold_in(jax.random.fold_in(streams_of[3], part), 71), part)
    orbitals = gaussian(own_keys[1], (N, N), N ** -0.5, 0.15625, ((0, 8),), jnp.float32)
    one_body = draw_one_body(jax.random.fold_in(jax.random.fold_in(streams_of[3], part), 71), part)
    return dict(chol_vectors=chol_vectors, orbitals=orbitals, one_body=one_body)


def rotate_one(matrix, orbitals):
    half = jnp.dot(matrix, orbitals, precision=lax.Precision.HIGHEST, preferred_element_type=jnp.float32)
    return jnp.dot(orbitals.T, half, precision=lax.Precision.HIGHEST, preferred_element_type=jnp.float32)


def reference(chol_vectors, orbitals, one_body):
    rotated = lax.map(lambda vector: rotate_one(vector, orbitals), chol_vectors)
    onebody_rot = rotate_one(one_body, orbitals)
    diagonals = jnp.diagonal(rotated, axis1=1, axis2=2)
    diag_mean = jnp.mean(diagonals * diagonals, axis=0)
    return rotated, onebody_rot, diag_mean
```

```python
import functools

import jax
import jax.numpy as jnp
from jax import lax
from jax.experimental import pallas as pl
from jax.experimental.pallas import tpu as pltpu
from jax.sharding import PartitionSpec as P

NT = (((1,), (1,)), ((), ()))
NN = (((1,), (0,)), ((), ()))


def split(value):
    high = value.astype(jnp.bfloat16)
    low = (value - high.astype(jnp.float32)).astype(jnp.bfloat16)
    return high, low


def dot3(a_high, a_low, b_high, b_low, dims):
    dot = functools.partial(
        lax.dot_general, dimension_numbers=dims, preferred_element_type=jnp.float32
    )
    return dot(a_high, b_high) + (dot(a_high, b_low) + dot(a_low, b_high))


def rotate_kernel(
    rows, subs, chol, hbody, coef, coef_t, rotated, onebody, diag,
    c_high, c_low, t_high, t_low, slot, x_high, x_low, out_buf,
    send, recv, h_send, h_recv,
    load_sem, store_sem, send_sem, recv_sem, h_send_sem, h_recv_sem,
):
    chunks, group, block, width = chol.shape
    n = rows * subs
    lanes = group * block
    h_lanes = h_send.shape[2]
    pieces = width // lanes
    row = lax.axis_index("row")
    sub = lax.axis_index("sub")
    me = row * subs + sub

    def place(index):
        return {"row": index // subs, "sub": lax.rem(index, subs)}

    barrier = pltpu.get_barrier_semaphore()

    def greet(step, carry):
        pl.semaphore_signal(
            barrier, inc=1, device_id=place(lax.rem(me + step, n)),
            device_id_type=pl.DeviceIdType.MESH,
        )
        return carry

    lax.fori_loop(1, n, greet, 0)

    def load(source):
        return pltpu.make_async_copy(source, slot, load_sem)

    for piece in range(pieces):
        copy = load(coef.at[piece])
        copy.start()
        copy.wait()
        for g in range(group):
            high, low = split(slot[g])
            at = pl.ds(piece * lanes + g * block, block)
            c_high[at, :] = high
            c_low[at, :] = low
    per = rows // pieces
    for piece in range(pieces):
        copy = load(coef_t.at[piece])
        copy.start()
        copy.wait()
        for r in range(per):
            part = slot[pl.ds(r * subs, subs)].reshape(subs * block, width)
            high, low = split(part)
            t_high[piece * per + r] = high
            t_low[piece * per + r] = low
    load(chol.at[0]).start()
    pl.semaphore_wait(barrier, n - 1)

    def message(c, index, mine):
        return pltpu.make_async_remote_copy(
            src_ref=send.at[c, index],
            dst_ref=recv.at[c, mine],
            send_sem=send_sem.at[c, index],
            recv_sem=recv_sem.at[c, mine],
            device_id=place(index),
            device_id_type=pl.DeviceIdType.MESH,
        )

    def h_message(index, mine):
        return pltpu.make_async_remote_copy(
            src_ref=h_send.at[index],
            dst_ref=h_recv.at[mine],
            send_sem=h_send_sem.at[index],
            recv_sem=h_recv_sem.at[mine],
            device_id=place(index),
            device_id_type=pl.DeviceIdType.MESH,
        )

    rest = jnp.zeros((h_lanes - block, width), jnp.float32)
    high = jnp.concatenate([hbody[...], rest], axis=0)
    high, low = split(high)
    x_high[pl.ds(0, h_lanes), :] = high
    x_low[pl.ds(0, h_lanes), :] = low

    def h_dest(step, carry):
        to_row = lax.rem(row + rows // 2 + step, rows)
        half = dot3(
            t_high[to_row], t_low[to_row],
            x_high[pl.ds(0, h_lanes), :], x_low[pl.ds(0, h_lanes), :], NT,
        )
        for s in range(subs):
            index = to_row * subs + s
            part = half[s * block:(s + 1) * block]

            @pl.when(index != me)
            def _():
                h_send[index] = part
                h_message(index, me).start()

            @pl.when(index == me)
            def _():
                h_recv[me] = part

        return carry

    lax.fori_loop(0, rows, h_dest, 0)

    def first_stage(c, carry):
        load(chol.at[c]).wait()
        for g in range(group):
            high, low = split(slot[g])
            at = pl.ds(g * block, block)
            if block % 16 == 0:
                x_high[at, :] = high
                x_low[at, :] = low
        if block % 16:
            high, low = split(slot[...].reshape(lanes, width))
            x_high[...] = high
            x_low[...] = low

        @pl.when(c + 1 < chunks)
        def _():
            load(chol.at[c + 1]).start()

        def dest(step, inner):
            to_row = lax.rem(row + rows // 2 + step, rows)
            half = dot3(t_high[to_row], t_low[to_row], x_high[...], x_low[...], NT)
            for s in range(subs):
                index = to_row * subs + s
                part = half[s * block:(s + 1) * block]

                @pl.when(index != me)
                def _():
                    send[c, index] = part
                    message(c, index, me).start()

                @pl.when(index == me)
                def _():
                    recv[c, me] = part

            return inner

        lax.fori_loop(0, rows, dest, 0)
        return carry

    lax.fori_loop(0, chunks, first_stage, 0)

    def h_arrive(step, carry):
        index = lax.rem(me + step, n)
        h_message(index, index).wait_recv()
        return carry

    lax.fori_loop(1, n, h_arrive, 0)
    for k in range(n):
        slot[0, :, k * block:(k + 1) * block] = h_recv[k, :, :block]
    high, low = split(slot[0])
    tile = 256
    for t in range(width // tile):
        at = pl.ds(t * tile, tile)
        onebody[:, at] = dot3(high, low, c_high[:, at], c_low[:, at], NN)

    diag[...] = jnp.zeros_like(diag)

    def second_stage(c, carry):
        def arrive(step, inner):
            index = lax.rem(me + step, n)
            message(c, index, index).wait_recv()
            return inner

        lax.fori_loop(1, n, arrive, 0)
        for g in range(group):
            for k in range(n):
                slot[g, :, k * block:(k + 1) * block] = (
                    recv[c, k, :, g * block:(g + 1) * block]
                )
        for g in range(group):
            high, low = split(slot[g])
            at = pl.ds(g * block, block)
            if block % 16 == 0:
                x_high[at, :] = high
                x_low[at, :] = low
        if block % 16:
            high, low = split(slot[...].reshape(lanes, width))
            x_high[...] = high
            x_low[...] = low

        def columns(t, inner):
            at = pl.ds(pl.multiple_of(t * tile, tile), tile)
            result = dot3(x_high[...], x_low[...], c_high[:, at], c_low[:, at], NN)
            out_buf[:, :, at] = result.reshape(group, block, tile)
            return inner

        lax.fori_loop(0, width // tile, columns, 0)
        copy = pltpu.make_async_copy(out_buf, rotated.at[c], store_sem)
        copy.start()
        own = (
            lax.broadcasted_iota(jnp.int32, (block, width), 1)
            == lax.broadcasted_iota(jnp.int32, (block, width), 0) + me * block
        )
        for g in range(group):
            picked = jnp.sum(jnp.where(own, out_buf[g], 0.0), axis=1, keepdims=True)
            diag[...] += jnp.broadcast_to(picked * picked, diag.shape)
        copy.wait()
        return carry

    lax.fori_loop(0, chunks, second_stage, 0)

    def drain(step, carry):
        index = lax.rem(me + step, n)
        h_message(index, me).wait_send()

        def each(c, inner):
            message(c, index, me).wait_send()
            return inner

        return lax.fori_loop(0, chunks, each, carry)

    lax.fori_loop(1, n, drain, 0)


def per_device(rows, subs, chol_vectors, orbitals, one_body):
    count, block, width = chol_vectors.shape
    n = rows * subs
    group = 1
    while (group * block) % 128 or count % group:
        group += 1
    lanes = group * block
    chunks = count // group
    pieces = width // lanes
    h_lanes = -(-block // 128) * 128
    full_orb = lax.all_gather(orbitals, ("row", "sub"), axis=0, tiled=True)
    coef = full_orb.reshape(pieces, group, block, width)
    coef_t = full_orb.T.reshape(pieces, group, block, width)
    flops = 2 * 6 * (count + 1) * block * width * width
    hbm = pl.BlockSpec(memory_space=pl.ANY)
    vmem = pl.BlockSpec(memory_space=pltpu.VMEM)
    bf16, f32 = jnp.bfloat16, jnp.float32
    rotated, onebody, diag = pl.pallas_call(
        functools.partial(rotate_kernel, rows, subs),
        out_shape=(
            jax.ShapeDtypeStruct((chunks, group, block, width), f32),
            jax.ShapeDtypeStruct((block, width), f32),
            jax.ShapeDtypeStruct((block, 128), f32),
        ),
        in_specs=[hbm, vmem, hbm, hbm],
        out_specs=(hbm, vmem, vmem),
        scratch_shapes=[
            pltpu.VMEM((width, width), bf16),
            pltpu.VMEM((width, width), bf16),
            pltpu.VMEM((rows, subs * block, width), bf16),
            pltpu.VMEM((rows, subs * block, width), bf16),
            pltpu.VMEM((group, block, width), f32),
            pltpu.VMEM((lanes, width), bf16),
            pltpu.VMEM((lanes, width), bf16),
            pltpu.VMEM((group, block, width), f32),
            pltpu.VMEM((chunks, n, block, lanes), f32),
            pltpu.VMEM((chunks, n, block, lanes), f32),
            pltpu.VMEM((n, block, h_lanes), f32),
            pltpu.VMEM((n, block, h_lanes), f32),
            pltpu.SemaphoreType.DMA,
            pltpu.SemaphoreType.DMA,
            pltpu.SemaphoreType.DMA((chunks, n)),
            pltpu.SemaphoreType.DMA((chunks, n)),
            pltpu.SemaphoreType.DMA((n,)),
            pltpu.SemaphoreType.DMA((n,)),
        ],
        compiler_params=pltpu.CompilerParams(
            collective_id=0, has_side_effects=True,
            vmem_limit_bytes=62 * 1024 * 1024,
        ),
        cost_estimate=pl.CostEstimate(
            flops=flops, bytes_accessed=8 * count * block * width, transcendentals=0
        ),
    )(chol_vectors.reshape(chunks, group, block, width), one_body, coef, coef_t)
    diag_total = lax.psum(diag[:, 0], "vec")
    diag_mean = diag_total / (count * lax.axis_size("vec"))
    return rotated.reshape(count, block, width), onebody, diag_mean


def solution(mesh):
    in_specs = (
        P(("grp", "vec"), ("row", "sub"), None),
        P(("grp", "row", "sub"), None),
        P(("grp", "row", "sub"), None),
    )
    out_specs = (
        P(("grp", "vec"), ("row", "sub"), None),
        P(("grp", "row", "sub"), None),
        P(("grp", "row", "sub")),
    )
    return jax.shard_map(
        functools.partial(per_device, mesh.shape["row"], mesh.shape["sub"]),
        mesh=mesh, in_specs=in_specs, out_specs=out_specs, check_vma=False,
    )
```

```python
import functools

import jax
import jax.numpy as jnp
from jax import lax
from jax.experimental import pallas as pl
from jax.experimental.pallas import tpu as pltpu
from jax.sharding import PartitionSpec as P

NT = (((1,), (1,)), ((), ()))
NN = (((1,), (0,)), ((), ()))


def split(value):
    high = value.astype(jnp.bfloat16)
    low = (value - high.astype(jnp.float32)).astype(jnp.bfloat16)
    return high, low


def dot3(a_high, a_low, b_high, b_low, dims):
    dot = functools.partial(
        lax.dot_general, dimension_numbers=dims, preferred_element_type=jnp.float32
    )
    return dot(a_high, b_high) + (dot(a_high, b_low) + dot(a_low, b_high))


def rotate_kernel(
    rows, subs, chol, hbody, coef, coef_t, rotated, onebody, diag,
    c_high, c_low, t_high, t_low, slot, x_high, x_low, out_buf,
    send, recv, h_send, h_recv,
    load_sem, store_sem, send_sem, recv_sem, h_send_sem, h_recv_sem,
):
    chunks, group, block, width = chol.shape
    n = rows * subs
    lanes = group * block
    h_lanes = h_send.shape[2]
    pieces = width // lanes
    row = lax.axis_index("row")
    sub = lax.axis_index("sub")
    me = row * subs + sub

    def place(index):
        return {"row": index // subs, "sub": lax.rem(index, subs)}

    barrier = pltpu.get_barrier_semaphore()

    def greet(step, carry):
        pl.semaphore_signal(
            barrier, inc=1, device_id=place(lax.rem(me + step, n)),
            device_id_type=pl.DeviceIdType.MESH,
        )
        return carry

    lax.fori_loop(1, n, greet, 0)

    def load(source):
        return pltpu.make_async_copy(source, slot, load_sem)

    for piece in range(pieces):
        copy = load(coef.at[piece])
        copy.start()
        copy.wait()
        for g in range(group):
            high, low = split(slot[g])
            at = pl.ds(piece * lanes + g * block, block)
            c_high[at, :] = high
            c_low[at, :] = low
    per = rows // pieces
    for piece in range(pieces):
        copy = load(coef_t.at[piece])
        copy.start()
        copy.wait()
        for r in range(per):
            part = slot[pl.ds(r * subs, subs)].reshape(subs * block, width)
            high, low = split(part)
            t_high[piece * per + r] = high
            t_low[piece * per + r] = low
    load(chol.at[0]).start()
    pl.semaphore_wait(barrier, n - 1)

    def message(c, index, mine):
        return pltpu.make_async_remote_copy(
            src_ref=send.at[c, index],
            dst_ref=recv.at[c, mine],
            send_sem=send_sem.at[c, index],
            recv_sem=recv_sem.at[c, mine],
            device_id=place(index),
            device_id_type=pl.DeviceIdType.MESH,
        )

    def h_message(index, mine):
        return pltpu.make_async_remote_copy(
            src_ref=h_send.at[index],
            dst_ref=h_recv.at[mine],
            send_sem=h_send_sem.at[index],
            recv_sem=h_recv_sem.at[mine],
            device_id=place(index),
            device_id_type=pl.DeviceIdType.MESH,
        )

    rest = jnp.zeros((h_lanes - block, width), jnp.float32)
    high = jnp.concatenate([hbody[...], rest], axis=0)
    high, low = split(high)
    x_high[pl.ds(0, h_lanes), :] = high
    x_low[pl.ds(0, h_lanes), :] = low

    def h_dest(step, carry):
        to_row = lax.rem(row + rows // 2 + step, rows)
        half = dot3(
            t_high[to_row], t_low[to_row],
            x_high[pl.ds(0, h_lanes), :], x_low[pl.ds(0, h_lanes), :], NT,
        )
        for s in range(subs):
            index = to_row * subs + s
            part = half[s * block:(s + 1) * block]

            @pl.when(index != me)
            def _():
                h_send[index] = part
                h_message(index, me).start()

            @pl.when(index == me)
            def _():
                h_recv[me] = part

        return carry

    lax.fori_loop(0, rows, h_dest, 0)

    def first_stage(c, carry):
        load(chol.at[c]).wait()
        for g in range(group):
            high, low = split(slot[g])
            at = pl.ds(g * block, block)
            if block % 16 == 0:
                x_high[at, :] = high
                x_low[at, :] = low
        if block % 16:
            high, low = split(slot[...].reshape(lanes, width))
            x_high[...] = high
            x_low[...] = low

        @pl.when(c + 1 < chunks)
        def _():
            load(chol.at[c + 1]).start()

        def dest(step, inner):
            to_row = lax.rem(row + rows // 2 + step, rows)
            half = dot3(t_high[to_row], t_low[to_row], x_high[...], x_low[...], NT)
            for s in range(subs):
                index = to_row * subs + s
                part = half[s * block:(s + 1) * block]

                @pl.when(index != me)
                def _():
                    send[c, index] = part
                    message(c, index, me).start()

                @pl.when(index == me)
                def _():
                    recv[c, me] = part

            return inner

        lax.fori_loop(0, rows, dest, 0)
        return carry

    lax.fori_loop(0, chunks, first_stage, 0)

    def h_arrive(step, carry):
        index = lax.rem(me + step, n)
        h_message(index, index).wait_recv()
        return carry

    lax.fori_loop(1, n, h_arrive, 0)
    for k in range(n):
        slot[0, :, k * block:(k + 1) * block] = h_recv[k, :, :block]
    high, low = split(slot[0])
    tile = 256
    for t in range(width // tile):
        at = pl.ds(t * tile, tile)
        onebody[:, at] = dot3(high, low, c_high[:, at], c_low[:, at], NN)

    diag[...] = jnp.zeros_like(diag)

    def second_stage(c, carry):
        def arrive(step, inner):
            index = lax.rem(me + step, n)
            message(c, index, index).wait_recv()
            return inner

        lax.fori_loop(1, n, arrive, 0)
        for g in range(group):
            for k in range(n):
                slot[g, :, k * block:(k + 1) * block] = (
                    recv[c, k, :, g * block:(g + 1) * block]
                )
        for g in range(group):
            high, low = split(slot[g])
            at = pl.ds(g * block, block)
            if block % 16 == 0:
                x_high[at, :] = high
                x_low[at, :] = low
        if block % 16:
            high, low = split(slot[...].reshape(lanes, width))
            x_high[...] = high
            x_low[...] = low

        def columns(t, inner):
            at = pl.ds(pl.multiple_of(t * tile, tile), tile)
            result = dot3(x_high[...], x_low[...], c_high[:, at], c_low[:, at], NN)
            out_buf[:, :, at] = result.reshape(group, block, tile)
            return inner

        lax.fori_loop(0, width // tile, columns, 0)
        copy = pltpu.make_async_copy(out_buf, rotated.at[c], store_sem)
        copy.start()
        own = (
            lax.broadcasted_iota(jnp.int32, (block, width), 1)
            == lax.broadcasted_iota(jnp.int32, (block, width), 0) + me * block
        )
        for g in range(group):
            picked = jnp.sum(jnp.where(own, out_buf[g], 0.0), axis=1, keepdims=True)
            diag[...] += jnp.broadcast_to(picked * picked, diag.shape)
        copy.wait()
        return carry

    lax.fori_loop(0, chunks, second_stage, 0)

    def drain(step, carry):
        index = lax.rem(me + step, n)
        h_message(index, me).wait_send()

        def each(c, inner):
            message(c, index, me).wait_send()
            return inner

        return lax.fori_loop(0, chunks, each, carry)

    lax.fori_loop(1, n, drain, 0)


def per_device(rows, subs, chol_vectors, orbitals, one_body):
    count, block, width = chol_vectors.shape
    n = rows * subs
    group = 1
    while (group * block) % 128 or count % group:
        group += 1
    lanes = group * block
    chunks = count // group
    pieces = width // lanes
    h_lanes = -(-block // 128) * 128
    share = block // lax.axis_size("vec")
    own = lax.dynamic_slice_in_dim(orbitals, lax.axis_index("vec") * share, share, 0)
    full_orb = lax.all_gather(own, ("row", "sub", "vec"), axis=0, tiled=True)
    coef = full_orb.reshape(pieces, group, block, width)
    coef_t = full_orb.T.reshape(pieces, group, block, width)
    flops = 2 * 6 * (count + 1) * block * width * width
    hbm = pl.BlockSpec(memory_space=pl.ANY)
    vmem = pl.BlockSpec(memory_space=pltpu.VMEM)
    bf16, f32 = jnp.bfloat16, jnp.float32
    rotated, onebody, diag = pl.pallas_call(
        functools.partial(rotate_kernel, rows, subs),
        out_shape=(
            jax.ShapeDtypeStruct((chunks, group, block, width), f32),
            jax.ShapeDtypeStruct((block, width), f32),
            jax.ShapeDtypeStruct((block, 128), f32),
        ),
        in_specs=[hbm, vmem, hbm, hbm],
        out_specs=(hbm, vmem, vmem),
        scratch_shapes=[
            pltpu.VMEM((width, width), bf16),
            pltpu.VMEM((width, width), bf16),
            pltpu.VMEM((rows, subs * block, width), bf16),
            pltpu.VMEM((rows, subs * block, width), bf16),
            pltpu.VMEM((group, block, width), f32),
            pltpu.VMEM((lanes, width), bf16),
            pltpu.VMEM((lanes, width), bf16),
            pltpu.VMEM((group, block, width), f32),
            pltpu.VMEM((chunks, n, block, lanes), f32),
            pltpu.VMEM((chunks, n, block, lanes), f32),
            pltpu.VMEM((n, block, h_lanes), f32),
            pltpu.VMEM((n, block, h_lanes), f32),
            pltpu.SemaphoreType.DMA,
            pltpu.SemaphoreType.DMA,
            pltpu.SemaphoreType.DMA((chunks, n)),
            pltpu.SemaphoreType.DMA((chunks, n)),
            pltpu.SemaphoreType.DMA((n,)),
            pltpu.SemaphoreType.DMA((n,)),
        ],
        compiler_params=pltpu.CompilerParams(
            collective_id=0, has_side_effects=True,
            vmem_limit_bytes=62 * 1024 * 1024,
        ),
        cost_estimate=pl.CostEstimate(
            flops=flops, bytes_accessed=8 * count * block * width, transcendentals=0
        ),
    )(chol_vectors.reshape(chunks, group, block, width), one_body, coef, coef_t)
    diag_total = lax.psum(diag[:, 0], "vec")
    diag_mean = diag_total / (count * lax.axis_size("vec"))
    return rotated.reshape(count, block, width), onebody, diag_mean


def solution(mesh):
    in_specs = (
        P(("grp", "vec"), ("row", "sub"), None),
        P(("grp", "row", "sub"), None),
        P(("grp", "row", "sub"), None),
    )
    out_specs = (
        P(("grp", "vec"), ("row", "sub"), None),
        P(("grp", "row", "sub"), None),
        P(("grp", "row", "sub")),
    )
    return jax.shard_map(
        functools.partial(per_device, mesh.shape["row"], mesh.shape["sub"]),
        mesh=mesh, in_specs=in_specs, out_specs=out_specs, check_vma=False,
    )
```
